512 devices in a mesh: blk: 128 (over z_hi, x, y), grp: 4 (over z_lo, core).
Axes of the slice: x: 4, y: 8, z: 8 (z_hi: 4, z_lo: 2; z = z_hi * 2 + z_lo), core: 2. Of those that a mesh axis runs over, the one named last changes fastest.
Arguments:
- embeddings: bfloat16 [131072, 1024], P(('blk', 'grp')), may hold values from -1 to 1
Outputs:
- density: float32 [131072], P(('blk', 'grp'))
The draws below stay inside these ranges and needn't reach their ends.
All inputs are finite; a program needn't handle non-finite values.
Results may differ from the reference program's by a relative error of at most 0.0003.
Values may be sent and summed in bfloat16 or wider, within the bound.
A program may use at most 64 MiB of HBM per device.

```python
import math
import jax
import jax.numpy as jnp
from jax import lax

D = 1024
BLOCK = 256
STOPS = 4
TOPICS = 64
PROTOS = 2048
NDOC = 131072
N_BLK = 128
N_GRP = 4


def draw_embeddings(key, part):
    key = jax.random.fold_in(key, 11)
    keys = jax.random.split(key, 5)
    proto_ids = jax.random.randint(keys[0], (NDOC,), 0, PROTOS)
    topic_ids = proto_ids % TOPICS
    topic_table = jax.random.truncated_normal(keys[1], -4.0, 4.0, (TOPICS, D), jnp.float32)
    proto_table = jax.random.truncated_normal(keys[2], -4.0, 4.0, (PROTOS, D), jnp.float32)
    noise = jax.random.truncated_normal(keys[3], -4.0, 4.0, (NDOC, D), jnp.float32)
    spread = jnp.exp(jax.random.uniform(keys[4], (NDOC, 1), jnp.float32, math.log(0.05), math.log(0.35)))
    mixed = 0.7 * jnp.take(topic_table, topic_ids, axis=0) + 0.7 * jnp.take(proto_table, proto_ids, axis=0) + spread * noise
    return (mixed * (1.0 / math.sqrt(D))).astype(jnp.bfloat16)


def setup_inputs(seed: int = 0) -> dict:
    seeds = jax.random.split(jax.random.key(seed), 2)
    embeddings = draw_embeddings(jax.random.fold_in(seeds[1], 71), 0)
    return {"embeddings": embeddings}


sharpness = 4.0


def affinity(queries, query_norms, targets, target_norms):
    products = jnp.dot(queries, targets.T, preferred_element_type=jnp.float32)
    distance = query_norms[:, None] + target_norms[None, :] - 2.0 * products
    return jnp.exp(-sharpness * distance)


def reference(embeddings):
    group_rows = N_GRP * BLOCK
    grouped = embeddings.reshape(N_BLK, group_rows, D)
    row_norms = jnp.sum(jnp.square(grouped.astype(jnp.float32)), axis=2)
    self_mask = jnp.arange(group_rows)[:, None] == jnp.arange(group_rows)[None, :]

    def visit(block_index, totals):
        queries = lax.dynamic_index_in_dim(grouped, block_index, 0, keepdims=False)
        query_norms = lax.dynamic_index_in_dim(row_norms, block_index, 0, keepdims=False)
        first = jnp.where(self_mask, jnp.float32(0.0), affinity(queries, query_norms, queries, query_norms))
        totals = totals.at[block_index].add(jnp.sum(first, axis=1))
        for stop_index in range(1, STOPS):
            source = (block_index - stop_index) % N_BLK
            targets = lax.dynamic_index_in_dim(grouped, source, 0, keepdims=False)
            target_norms = lax.dynamic_index_in_dim(row_norms, source, 0, keepdims=False)
            kernel = affinity(queries, query_norms, targets, target_norms)
            totals = totals.at[block_index].add(jnp.sum(kernel, axis=1))
            totals = totals.at[source].add(jnp.sum(kernel, axis=0))
        return totals

    totals = lax.fori_loop(0, N_BLK, visit, jnp.zeros((N_BLK, group_rows), jnp.float32))
    return jnp.log1p(totals.reshape(-1))
```

```python
import functools
import math

import jax
import jax.numpy as jnp
from jax import lax
from jax.experimental import pallas as pl
from jax.experimental.pallas import tpu as pltpu
from jax.sharding import PartitionSpec as P

MESH = pl.DeviceIdType.MESH
SHARPNESS = 4.0
LOG2E = math.log2(math.e)
SCALE = SHARPNESS * LOG2E
CHUNKS = 4
PERIOD = 32

OWN, CROSS, PREV, XPREV = 0, 2, 4, 6


def kernel(n_blk, block, width, x, out, rows, nxt, nxt2, relay, rsum, rnorm, ncol, ncol2, gains, lsem, ssem, rsem):
    p = lax.axis_index("blk")
    g = lax.axis_index("grp")
    h = g // 2
    c = lax.rem(g, 2)
    m = lax.rem(p, PERIOD)
    is_a, is_b = h == 0, h == 1
    first, low, last, high = m == 0, m < 2, m == PERIOD - 1, m >= PERIOD - 2
    has_prev = jnp.logical_not(jnp.logical_and(first, is_b))
    has_nxt = jnp.logical_not(jnp.logical_and(high, is_a))
    has_nxt2 = jnp.logical_or(jnp.logical_and(first, is_a), jnp.logical_and(high, is_b))
    not_last, not_low = jnp.logical_not(last), jnp.logical_not(low)
    low_a, low_b = jnp.logical_and(low, is_a), jnp.logical_and(low, is_b)
    high_a, high_b = jnp.logical_and(high, is_a), jnp.logical_and(high, is_b)
    last_b = jnp.logical_and(last, is_b)
    send_xprev = jnp.logical_or(not_last, is_b)
    send_nxt2 = jnp.logical_or(jnp.logical_and(m == 2, is_b), low_a)
    first_a = jnp.logical_and(first, is_a)
    first_b = jnp.logical_and(first, is_b)

    def dev(dp, hh, cc):
        return (lax.rem(p + dp + n_blk, n_blk), hh * 2 + cc)

    step = block // CHUNKS

    def part(ref, i):
        return ref.at[pl.ds(i * step, step)]

    sems = [0]

    def flow(count):
        base = sems[0]
        sems[0] += count
        return base

    def copy(src, dst, k, device, ks=None):
        return pltpu.make_async_remote_copy(
            src_ref=src, dst_ref=dst, send_sem=ssem.at[k if ks is None else ks], recv_sem=rsem.at[k],
            device_id=device, device_id_type=MESH)

    f_own = flow(1)
    f_cross, f_crossf, f_prev, f_prevf = flow(CHUNKS), flow(CHUNKS), flow(CHUNKS), flow(CHUNKS)
    f_xprev, f_xprevf, f_nxt, f_nxt2, f_relay = flow(CHUNKS), flow(CHUNKS), flow(CHUNKS), flow(CHUNKS), flow(CHUNKS)
    f_gain = flow(10)

    core = dev(0, h, 1 - c)
    parts = range(CHUNKS)
    own_copy = copy(x, rows.at[OWN + c], f_own, core)
    cross = [copy(part(x, i), part(rows.at[CROSS + c], i), f_cross + i, dev(0, 1 - h, c)) for i in parts]
    crossf = [copy(part(rows.at[CROSS + c], i), part(rows.at[CROSS + c], i), f_crossf + i, core) for i in parts]
    prev = [copy(part(x, i), part(rows.at[PREV + c], i), f_prev + i, dev(1, h, c)) for i in parts]
    prev_relay = [copy(part(rows.at[CROSS + c], i), part(rows.at[PREV + c], i), f_prev + i, dev(1, 0, c)) for i in parts]
    prevf = [copy(part(rows.at[PREV + c], i), part(rows.at[PREV + c], i), f_prevf + i, core) for i in parts]
    xprev = [copy(part(x, i), part(rows.at[XPREV + c], i), f_xprev + i, dev(1, 1 - h, c)) for i in parts]
    xprevf = [copy(part(rows.at[XPREV + c], i), part(rows.at[XPREV + c], i), f_xprevf + i, core) for i in parts]
    nxtc = [copy(part(x, i), part(nxt, i), f_nxt + i, dev(-2, h, c)) for i in parts]
    nxt_relay = [copy(part(relay, i), part(nxt, i), f_nxt + i, dev(PERIOD - 2, 1, c)) for i in parts]
    to_relay = [copy(part(rows.at[CROSS + c], i), part(relay, i), f_relay + i, dev(-PERIOD, 1, c)) for i in parts]
    nxt2c = [copy(part(x, i), part(nxt2, i), f_nxt2 + i, dev(-2, 1 - h, c)) for i in parts]

    local = pltpu.make_async_copy(x, rows.at[OWN + c], lsem)
    local.start()

    barrier = pltpu.get_barrier_semaphore()

    def hello(device):
        pl.semaphore_signal(barrier, inc=1, device_id=device, device_id_type=MESH)

    hello(core)
    hello(dev(0, 1 - h, c))
    pl.when(jnp.logical_not(first))(lambda: hello(dev(-1, h, c)))
    pl.when(has_prev)(lambda: hello(dev(-1, 1 - h, c)))
    pl.when(jnp.logical_not(high))(lambda: hello(dev(2, h, c)))
    pl.when(high_b)(lambda: hello(dev(-(PERIOD - 2), 1, c)))
    pl.when(low_b)(lambda: hello(dev(PERIOD, 0, c)))
    pl.when(has_nxt2)(lambda: hello(dev(2, 1 - h, c)))

    def one(flag):
        return jnp.where(flag, 1, 0)

    targets = 2 + one(not_last) + one(send_xprev) + 1 + one(send_nxt2)
    pl.semaphore_wait(barrier, targets)

    for i in parts:
        cross[i].start()
        pl.when(not_last)(prev[i].start)
        pl.when(not_low)(nxtc[i].start)
        pl.when(send_nxt2)(nxt2c[i].start)
        if i == 0:
            own_copy.start()
    for i in parts:
        pl.when(send_xprev)(xprev[i].start)

    rsum[...] = jnp.zeros_like(rsum)

    def squares(block_rows):
        v = block_rows.astype(jnp.float32)
        v = v * v
        total = v[:, 0:128]
        for k in range(1, width // 128):
            total = total + v[:, k * 128:(k + 1) * 128]
        return total

    def flat(acc, weight):
        ones = jnp.full((8, 128), weight, jnp.float32)
        return lax.dot_general(ones, acc, (((1,), (1,)), ((), ())), precision=lax.Precision.HIGHEST,
                               preferred_element_type=jnp.float32)

    def norms(s):
        rnorm[s] = flat(squares(rows[s]), 1.0) * SCALE

    def column_norms(block_rows):
        return jnp.sum(squares(block_rows), axis=1, keepdims=True) * SCALE

    def affinity(targets_, target_norms, s):
        products = lax.dot_general(targets_, rows[s], (((1,), (1,)), ((), ())), preferred_element_type=jnp.float32)
        return jnp.exp2(products * (2.0 * SCALE) - (target_norms + rnorm[s, 0:1, :]))

    def fold(e):
        total = e[:, 0:128]
        for k in range(1, block // 128):
            total = total + e[:, k * 128:(k + 1) * 128]
        return total

    def sweep(ref, lo, hi):
        target = ref[...]
        target_norms = column_norms(target)

        def visit(s, acc):
            e = affinity(target, target_norms, s)
            rsum[s] += jnp.sum(e.reshape(block // 8, 8, block), axis=0)
            return acc + fold(e)

        acc = lax.fori_loop(lo, hi, visit, jnp.zeros((block, 128), jnp.float32))
        return flat(acc, 0.125)

    local.wait()
    norms(OWN + c)

    for i in parts:
        cross[i].wait_recv()
        crossf[i].start()
        pl.when(low_a)(to_relay[i].start)
        pl.when(last_b)(prev_relay[i].start)

    @pl.when(low_b)
    def _():
        for i in parts:
            to_relay[i].wait_recv()
            nxt_relay[i].start()

    @pl.when(has_prev)
    def _():
        for i in parts:
            prev[i].wait_recv()
            prevf[i].start()

    own_copy.wait_recv()
    norms(OWN + 1 - c)
    for i in parts:
        crossf[i].wait_recv()
    norms(CROSS)
    norms(CROSS + 1)

    mine = rows[OWN + c]
    mine_norms = column_norms(mine)
    diagonal = lax.broadcasted_iota(jnp.int32, (block, block), 0) == lax.broadcasted_iota(jnp.int32, (block, block), 1)

    def visit_own(s, acc):
        e = affinity(mine, mine_norms, s)
        e = jnp.where(jnp.logical_and(diagonal, s == OWN + c), 0.0, e)
        return acc + fold(e)

    acc = lax.fori_loop(0, 4, visit_own, jnp.zeros((block, 128), jnp.float32))
    rsum[OWN + c] += flat(acc, 0.125)

    @pl.when(has_prev)
    def _():
        for i in parts:
            prevf[i].wait_recv()
        norms(PREV)
        norms(PREV + 1)

        @pl.when(jnp.logical_not(high_b))
        def _():
            rsum[PREV + c] += sweep(rows.at[PREV + c], 0, 4)

        for i in parts:
            xprev[i].wait_recv()
            xprevf[i].start()
        for i in parts:
            xprevf[i].wait_recv()
        norms(XPREV)
        norms(XPREV + 1)

        @pl.when(jnp.logical_or(first_a, high_a))
        def _():
            rsum[XPREV + c] += sweep(rows.at[XPREV + c], 0, 4)

    @pl.when(has_nxt)
    def _():
        for i in parts:
            nxtc[i].wait_recv()
        ncol[...] = sweep(nxt, 0, jnp.where(first_b, 4, 8))

    @pl.when(has_nxt2)
    def _():
        for i in parts:
            nxt2c[i].wait_recv()
        ncol2[...] = sweep(nxt2, jnp.where(first, 4, 0), 8)

    def gain(src, slot, device, ks):
        return copy(src, gains.at[slot], f_gain + slot, device, f_gain + ks)

    g_own = [gain(rsum.at[OWN + 1 - c], 0, core, 0)]
    g_own += [gain(rsum.at[CROSS + k], 1 + c, dev(0, 1 - h, k), 1 + k) for k in range(2)]
    g_prev = [gain(rsum.at[PREV + k], 3 + c, dev(-1, h, k), 3 + k) for k in range(2)]
    g_prev += [gain(rsum.at[XPREV + k], 5 + c, dev(-1, 1 - h, k), 5 + k) for k in range(2)]
    g_nxt = gain(ncol, 7, dev(2, h, c), 7)
    g_nxt2 = gain(ncol2, 8, dev(2, 1 - h, c), 8)

    pl.when(has_nxt)(g_nxt.start)
    pl.when(has_nxt2)(g_nxt2.start)

    @pl.when(has_prev)
    def _():
        for q in g_prev:
            q.start()

    for q in g_own:
        q.start()

    def arrive(slot):
        copy(gains.at[slot], gains.at[slot], f_gain + slot, core).wait_recv()
        rsum[OWN + c] += gains[slot]

    for slot in range(3):
        arrive(slot)

    @pl.when(jnp.logical_or(not_last, is_a))
    def _():
        arrive(3)
        arrive(4)

    @pl.when(jnp.logical_or(not_last, is_b))
    def _():
        arrive(5)
        arrive(6)

    pl.when(jnp.logical_not(low_a))(lambda: arrive(7))
    pl.when(send_nxt2)(lambda: arrive(8))

    out[...] = jnp.log1p(jnp.sum(rsum[OWN + c], axis=0, keepdims=True))

    own_copy.wait_send()
    for i in parts:
        cross[i].wait_send()
        crossf[i].wait_send()
        pl.when(not_last)(prev[i].wait_send)
        pl.when(last_b)(prev_relay[i].wait_send)
        pl.when(has_prev)(prevf[i].wait_send)
        pl.when(send_xprev)(xprev[i].wait_send)
        pl.when(has_prev)(xprevf[i].wait_send)
        pl.when(not_low)(nxtc[i].wait_send)
        pl.when(low_b)(nxt_relay[i].wait_send)
        pl.when(low_a)(to_relay[i].wait_send)
        pl.when(send_nxt2)(nxt2c[i].wait_send)
    for q in g_own:
        q.wait_send()

    @pl.when(has_prev)
    def _():
        for q in g_prev:
            q.wait_send()

    pl.when(has_nxt)(g_nxt.wait_send)
    pl.when(has_nxt2)(g_nxt2.wait_send)


def solution(mesh):
    n_blk = mesh.shape["blk"]

    def body(embeddings):
        block, width = embeddings.shape
        n_sem = 1 + 9 * CHUNKS + 10
        sums = pl.pallas_call(
            functools.partial(kernel, n_blk, block, width),
            out_shape=jax.ShapeDtypeStruct((1, block), jnp.float32),
            in_specs=[pl.BlockSpec(memory_space=pl.ANY)],
            out_specs=pl.BlockSpec(memory_space=pltpu.VMEM),
            scratch_shapes=[
                pltpu.VMEM((8, block, width), jnp.bfloat16),
                pltpu.VMEM((block, width), jnp.bfloat16),
                pltpu.VMEM((block, width), jnp.bfloat16),
                pltpu.VMEM((block, width), jnp.bfloat16),
                pltpu.VMEM((8, 8, block), jnp.float32),
                pltpu.VMEM((8, 8, block), jnp.float32),
                pltpu.VMEM((8, block), jnp.float32),
                pltpu.VMEM((8, block), jnp.float32),
                pltpu.VMEM((9, 8, block), jnp.float32),
                pltpu.SemaphoreType.DMA,
                pltpu.SemaphoreType.DMA((n_sem,)),
                pltpu.SemaphoreType.DMA((n_sem,)),
            ],
            compiler_params=pltpu.CompilerParams(
                collective_id=0, has_side_effects=True, vmem_limit_bytes=40 * 2**20
            ),
            cost_estimate=pl.CostEstimate(flops=2 * 16 * block * block * width, bytes_accessed=2 * block * width,
                                          transcendentals=16 * block * block),
        )(embeddings)
        return sums.reshape(block)

    return jax.shard_map(
        body, mesh=mesh, in_specs=(P(("blk", "grp"), None),), out_specs=P(("blk", "grp")), check_vma=False
    )
```

```python
import functools
import math

import jax
import jax.numpy as jnp
from jax import lax
from jax.experimental import pallas as pl
from jax.experimental.pallas import tpu as pltpu
from jax.sharding import PartitionSpec as P

MESH = pl.DeviceIdType.MESH
SHARPNESS = 4.0
LOG2E = math.log2(math.e)
SCALE = SHARPNESS * LOG2E
CHUNKS = 4
RELAYED = 3
PERIOD = 32

OWN, CROSS, PREV, XPREV = 0, 2, 4, 6


def kernel(n_blk, block, width, x, out, rows, nxt, nxt2, relay, rsum, rnorm, ncol, ncol2, gains, lsem, ssem, rsem):
    p = n_blk - 1 - lax.axis_index("blk")
    g = lax.axis_index("grp")
    h = 1 - g // 2
    c = lax.rem(g, 2)
    m = lax.rem(p, PERIOD)
    is_a, is_b = h == 0, h == 1
    first, low, last, high = m == 0, m < 2, m == PERIOD - 1, m >= PERIOD - 2
    has_prev = jnp.logical_not(jnp.logical_and(first, is_b))
    has_nxt = jnp.logical_not(jnp.logical_and(high, is_a))
    has_nxt2 = jnp.logical_or(jnp.logical_and(first, is_a), jnp.logical_and(high, is_b))
    not_last, not_low = jnp.logical_not(last), jnp.logical_not(low)
    low_a, low_b = jnp.logical_and(low, is_a), jnp.logical_and(low, is_b)
    high_a, high_b = jnp.logical_and(high, is_a), jnp.logical_and(high, is_b)
    last_b = jnp.logical_and(last, is_b)
    inner = jnp.logical_not(first)
    first_a = jnp.logical_and(first, is_a)
    first_b = jnp.logical_and(first, is_b)
    second_b = jnp.logical_and(m == 2, is_b)

    def dev(dp, hh, cc):
        return (n_blk - 1 - lax.rem(p + dp + n_blk, n_blk), (1 - hh) * 2 + cc)

    step = block // CHUNKS

    def part(ref, i):
        return ref.at[pl.ds(i * step, step)]

    sems = [0]

    def flow(count):
        base = sems[0]
        sems[0] += count
        return base

    def copy(src, dst, k, device, ks=None):
        return pltpu.make_async_remote_copy(
            src_ref=src, dst_ref=dst, send_sem=ssem.at[k if ks is None else ks], recv_sem=rsem.at[k],
            device_id=device, device_id_type=MESH)

    f_own = flow(1)
    f_cross, f_crossf, f_prev, f_prevf = flow(CHUNKS), flow(CHUNKS), flow(CHUNKS), flow(CHUNKS)
    f_xprev, f_xprevf, f_nxt, f_nxt2, f_relay = flow(CHUNKS), flow(CHUNKS), flow(CHUNKS), flow(CHUNKS), flow(CHUNKS)
    f_gain = flow(10)

    core = dev(0, h, 1 - c)
    parts = range(CHUNKS)
    own_copy = copy(x, rows.at[OWN + c], f_own, core)
    cross = [copy(part(x, i), part(rows.at[CROSS + c], i), f_cross + i, dev(0, 1 - h, c)) for i in parts]
    crossf = [copy(part(rows.at[CROSS + c], i), part(rows.at[CROSS + c], i), f_crossf + i, core) for i in parts]
    prev = [copy(part(x, i), part(rows.at[PREV + c], i), f_prev + i, dev(1, h, c)) for i in parts]
    prev_relay = [copy(part(rows.at[CROSS + c], i), part(rows.at[PREV + c], i), f_prev + i, dev(1, 0, c)) for i in parts]
    prevf = [copy(part(rows.at[PREV + c], i), part(rows.at[PREV + c], i), f_prevf + i, core) for i in parts]
    xprev = [copy(part(rows.at[PREV + c], i), part(rows.at[XPREV + c], i), f_xprev + i, dev(0, 1 - h, c)) for i in parts]
    xprev_own = [copy(part(x, i), part(rows.at[XPREV + c], i), f_xprev + i, dev(1, 0, c)) for i in parts]
    xprevf = [copy(part(rows.at[XPREV + c], i), part(rows.at[XPREV + c], i), f_xprevf + i, core) for i in parts]
    nxtc = [copy(part(x, i), part(nxt, i), f_nxt + i, dev(-2, h, c)) for i in parts]
    nxt_relay = [copy(part(relay, i), part(nxt, i), f_nxt + i, dev(PERIOD - 2, 1, c)) for i in parts[:RELAYED]]
    to_relay = [copy(part(rows.at[CROSS + c], i), part(relay, i), f_relay + i, dev(-PERIOD, 1, c)) for i in parts[:RELAYED]]
    to_relay += [copy(part(rows.at[CROSS + c], i), part(nxt, i), f_nxt + i, dev(-2, 1, c)) for i in parts[RELAYED:]]
    nxt2_relay = [copy(part(nxt, i), part(nxt2, i), f_nxt2 + i, dev(0, 0, c)) for i in parts]
    nxt2c = [copy(part(x, i), part(nxt2, i), f_nxt2 + i, dev(-2, 1 - h, c)) for i in parts]

    local = pltpu.make_async_copy(x, rows.at[OWN + c], lsem)
    local.start()

    barrier = pltpu.get_barrier_semaphore()

    def hello(device):
        pl.semaphore_signal(barrier, inc=1, device_id=device, device_id_type=MESH)

    hello(core)
    hello(dev(0, 1 - h, c))
    pl.when(jnp.logical_not(first))(lambda: hello(dev(-1, h, c)))
    pl.when(first_a)(lambda: hello(dev(-1, 1, c)))
    pl.when(jnp.logical_not(high))(lambda: hello(dev(2, h, c)))
    pl.when(high_b)(lambda: hello(dev(-(PERIOD - 2), 1, c)))
    pl.when(low_b)(lambda: hello(dev(PERIOD, 0, c)))
    pl.when(high_b)(lambda: hello(dev(2, 0, c)))

    def one(flag):
        return jnp.where(flag, 1, 0)

    targets = 2 + one(not_last) + one(last_b) + 1 + one(low_a)
    pl.semaphore_wait(barrier, targets)

    for i in parts:
        cross[i].start()
        pl.when(not_last)(prev[i].start)
        pl.when(not_low)(nxtc[i].start)
        pl.when(low_a)(nxt2c[i].start)
        pl.when(last_b)(xprev_own[i].start)
        if i == 0:
            own_copy.start()

    rsum[...] = jnp.zeros_like(rsum)

    def squares(block_rows):
        v = block_rows.astype(jnp.float32)
        v = v * v
        total = v[:, 0:128]
        for k in range(1, width // 128):
            total = total + v[:, k * 128:(k + 1) * 128]
        return total

    def flat(acc, weight):
        ones = jnp.full((8, 128), weight, jnp.float32)
        return lax.dot_general(ones, acc, (((1,), (1,)), ((), ())), precision=lax.Precision.HIGHEST,
                               preferred_element_type=jnp.float32)

    def norms(s):
        rnorm[s] = flat(squares(rows[s]), 1.0) * SCALE

    def column_norms(block_rows):
        return jnp.sum(squares(block_rows), axis=1, keepdims=True) * SCALE

    def affinity(targets_, target_norms, s):
        products = lax.dot_general(targets_, rows[s], (((1,), (1,)), ((), ())), preferred_element_type=jnp.float32)
        return jnp.exp2(products * (2.0 * SCALE) - (target_norms + rnorm[s, 0:1, :]))

    def fold(e):
        total = e[:, 0:128]
        for k in range(1, block // 128):
            total = total + e[:, k * 128:(k + 1) * 128]
        return total

    def sweep(target, target_norms, slots, acc):
        for t in slots:
            e = affinity(target, target_norms, t)
            rsum[t] += jnp.sum(e.reshape(block // 8, 8, block), axis=0)
            acc = acc + fold(e)
        return acc

    def whole(ref, slots):
        target = ref[...]
        return flat(sweep(target, column_norms(target), slots, jnp.zeros((block, 128), jnp.float32)), 0.125)

    local.wait()
    norms(OWN + c)

    def pass_relay(i):
        to_relay[i].wait_recv()
        nxt_relay[i].start()

    def pass_prev(i):
        prev[i].wait_recv()
        prevf[i].start()

    def pass_both(i):
        pass_prev(i)
        xprev[i].start()

    for i in parts:
        cross[i].wait_recv()
        pl.when(low_a)(to_relay[i].start)
        pl.when(last_b)(prev_relay[i].start)
        crossf[i].start()
        pl.when(inner)(functools.partial(pass_both, i))
        if i >= 1:
            pl.when(low_b)(functools.partial(pass_relay, i - 1))

    own_copy.wait_recv()
    norms(OWN + 1 - c)
    for i in parts:
        crossf[i].wait_recv()
    norms(CROSS)
    norms(CROSS + 1)

    mine = rows[OWN + c]
    mine_norms = column_norms(mine)
    diagonal = lax.broadcasted_iota(jnp.int32, (block, block), 0) == lax.broadcasted_iota(jnp.int32, (block, block), 1)

    acc = jnp.zeros((block, 128), jnp.float32)
    for t in range(4):
        e = affinity(mine, mine_norms, t)
        if t < 2:
            e = jnp.where(jnp.logical_and(diagonal, c == t), 0.0, e)
        acc = acc + fold(e)
    rsum[OWN + c] += flat(acc, 0.125)

    def get_prev():
        for i in parts:
            prevf[i].wait_recv()
        norms(PREV)
        norms(PREV + 1)

    def pass_xprev(some):
        for i in some:
            xprev[i].wait_recv()
            xprevf[i].start()

    def get_xprev():
        for i in parts:
            xprevf[i].wait_recv()
        norms(XPREV)
        norms(XPREV + 1)

    def get_nxt():
        for i in parts:
            nxtc[i].wait_recv()
        target = nxt[...]
        return target, column_norms(target), jnp.zeros((block, 128), jnp.float32)

    @pl.when(inner)
    def _():
        get_prev()

        @pl.when(jnp.logical_not(high_b))
        def _():
            rsum[PREV + c] += whole(rows.at[PREV + c], range(4))

    @pl.when(jnp.logical_and(inner, jnp.logical_not(high)))
    def _():
        pass_xprev(parts[:-1])
        target, target_norms, acc = get_nxt()
        acc = sweep(target, target_norms, range(4), acc)
        pass_xprev(parts[-1:])
        acc = sweep(target, target_norms, range(4, 6), acc)
        get_xprev()
        ncol[...] = flat(sweep(target, target_norms, range(6, 8), acc), 0.125)

    @pl.when(first_b)
    def _():
        for i in parts:
            nxtc[i].wait_recv()
            nxt2_relay[i].start()
        ncol[...] = whole(nxt, range(4))

    @pl.when(first_a)
    def _():
        target, target_norms, acc = get_nxt()
        acc = sweep(target, target_norms, range(4), acc)
        pass_xprev(parts)
        for i in parts:
            pass_prev(i)
        get_xprev()
        rsum[XPREV + c] += whole(rows.at[XPREV + c], range(4))
        acc = sweep(target, target_norms, range(6, 8), acc)
        get_prev()
        rsum[PREV + c] += whole(rows.at[PREV + c], range(4))
        ncol[...] = flat(sweep(target, target_norms, range(4, 6), acc), 0.125)
        for i in parts:
            nxt2c[i].wait_recv()
        ncol2[...] = whole(nxt2, range(PREV, 8))

    @pl.when(high_a)
    def _():
        pass_xprev(parts)
        get_xprev()
        rsum[XPREV + c] += whole(rows.at[XPREV + c], range(4))

    @pl.when(high_b)
    def _():
        pass_xprev(parts)
        get_xprev()
        for i in parts:
            nxt2c[i].wait_recv()
        ncol2[...] = whole(nxt2, range(8))
        target, target_norms, acc = get_nxt()
        ncol[...] = flat(sweep(target, target_norms, range(8), acc), 0.125)

    def gain(src, slot, device, ks):
        return copy(src, gains.at[slot], f_gain + slot, device, f_gain + ks)

    g_own = [gain(rsum.at[OWN + 1 - c], 0, core, 0)]
    g_own += [gain(rsum.at[CROSS + k], 1 + c, dev(0, 1 - h, k), 1 + k) for k in range(2)]
    g_prev = [gain(rsum.at[PREV + k], 3 + c, dev(-1, h, k), 3 + k) for k in range(2)]
    g_prev += [gain(rsum.at[XPREV + k], 5 + c, dev(-1, 1 - h, k), 5 + k) for k in range(2)]
    g_nxt = gain(ncol, 7, dev(2, h, c), 7)
    g_nxt2 = gain(ncol2, 8, dev(2, 1 - h, c), 8)

    pl.when(has_nxt)(g_nxt.start)
    pl.when(has_nxt2)(g_nxt2.start)

    @pl.when(has_prev)
    def _():
        for q in g_prev:
            q.start()

    for q in g_own:
        q.start()

    def arrive(slot):
        copy(gains.at[slot], gains.at[slot], f_gain + slot, core).wait_recv()
        rsum[OWN + c] += gains[slot]

    for slot in range(3):
        arrive(slot)

    @pl.when(jnp.logical_or(not_last, is_a))
    def _():
        arrive(3)
        arrive(4)

    @pl.when(jnp.logical_or(not_last, is_b))
    def _():
        arrive(5)
        arrive(6)

    pl.when(jnp.logical_not(low_a))(lambda: arrive(7))
    pl.when(jnp.logical_or(low_a, second_b))(lambda: arrive(8))

    out[...] = jnp.log1p(jnp.sum(rsum[OWN + c], axis=0, keepdims=True))

    own_copy.wait_send()
    for i in parts:
        cross[i].wait_send()
        crossf[i].wait_send()
        pl.when(not_last)(prev[i].wait_send)
        pl.when(last_b)(prev_relay[i].wait_send)
        pl.when(has_prev)(prevf[i].wait_send)
        pl.when(inner)(xprev[i].wait_send)
        pl.when(last_b)(xprev_own[i].wait_send)
        pl.when(has_prev)(xprevf[i].wait_send)
        pl.when(not_low)(nxtc[i].wait_send)
        if i < RELAYED:
            pl.when(low_b)(nxt_relay[i].wait_send)
        pl.when(low_a)(to_relay[i].wait_send)
        pl.when(low_a)(nxt2c[i].wait_send)
        pl.when(first_b)(nxt2_relay[i].wait_send)
    for q in g_own:
        q.wait_send()

    @pl.when(has_prev)
    def _():
        for q in g_prev:
            q.wait_send()

    pl.when(has_nxt)(g_nxt.wait_send)
    pl.when(has_nxt2)(g_nxt2.wait_send)


def solution(mesh):
    n_blk = mesh.shape["blk"]

    def body(embeddings):
        block, width = embeddings.shape
        n_sem = 1 + 9 * CHUNKS + 10
        sums = pl.pallas_call(
            functools.partial(kernel, n_blk, block, width),
            out_shape=jax.ShapeDtypeStruct((1, block), jnp.float32),
            in_specs=[pl.BlockSpec(memory_space=pl.ANY)],
            out_specs=pl.BlockSpec(memory_space=pltpu.VMEM),
            scratch_shapes=[
                pltpu.VMEM((8, block, width), jnp.bfloat16),
                pltpu.VMEM((block, width), jnp.bfloat16),
                pltpu.VMEM((block, width), jnp.bfloat16),
                pltpu.VMEM((block, width), jnp.bfloat16),
                pltpu.VMEM((8, 8, block), jnp.float32),
                pltpu.VMEM((8, 8, block), jnp.float32),
                pltpu.VMEM((8, block), jnp.float32),
                pltpu.VMEM((8, block), jnp.float32),
                pltpu.VMEM((9, 8, block), jnp.float32),
                pltpu.SemaphoreType.DMA,
                pltpu.SemaphoreType.DMA((n_sem,)),
                pltpu.SemaphoreType.DMA((n_sem,)),
            ],
            compiler_params=pltpu.CompilerParams(
                collective_id=0, has_side_effects=True, vmem_limit_bytes=40 * 2**20
            ),
            cost_estimate=pl.CostEstimate(flops=2 * 16 * block * block * width, bytes_accessed=2 * block * width,
                                          transcendentals=16 * block * block),
        )(embeddings)
        return sums.reshape(block)

    return jax.shard_map(
        body, mesh=mesh, in_specs=(P(("blk", "grp"), None),), out_specs=P(("blk", "grp")), check_vma=False
    )
```

```python
import functools
import math

import jax
import jax.numpy as jnp
from jax import lax
from jax.experimental import pallas as pl
from jax.experimental.pallas import tpu as pltpu
from jax.sharding import PartitionSpec as P

MESH = pl.DeviceIdType.MESH
SHARPNESS = 4.0
LOG2E = math.log2(math.e)
SCALE = SHARPNESS * LOG2E
CHUNKS = 4
PREV_CUT, XPREV_CUT, NXT_CUT = 0, 2, 2
PERIOD = 32
ROW = 8

OWN, CROSS, PREV, XPREV = 0, 2, 4, 6


def kernel(n_blk, block, width, x, out, rows, nxt, nxt2, relay, rsum, rnorm, ncol, ncol2, gains, lsem, ssem, rsem):
    p = n_blk - 1 - lax.axis_index("blk")
    g = lax.axis_index("grp")
    h = 1 - g // 2
    c = lax.rem(g, 2)
    m = lax.rem(p, PERIOD)
    is_a, is_b = h == 0, h == 1
    first, low, last, high = m == 0, m < 2, m == PERIOD - 1, m >= PERIOD - 2
    has_prev = jnp.logical_not(jnp.logical_and(first, is_b))
    has_nxt = jnp.logical_not(jnp.logical_and(high, is_a))
    has_nxt2 = jnp.logical_or(jnp.logical_and(first, is_a), jnp.logical_and(high, is_b))
    not_last, not_low = jnp.logical_not(last), jnp.logical_not(low)
    turn_a = jnp.logical_and(m == ROW - 1, is_a)
    low_a, low_b = jnp.logical_and(low, is_a), jnp.logical_and(low, is_b)
    high_a, high_b = jnp.logical_and(high, is_a), jnp.logical_and(high, is_b)
    last_a, last_b = jnp.logical_and(last, is_a), jnp.logical_and(last, is_b)
    inner = jnp.logical_not(first)
    first_a = jnp.logical_and(first, is_a)
    first_b = jnp.logical_and(first, is_b)
    second_b = jnp.logical_and(m == 2, is_b)

    def dev(dp, hh, cc):
        return (n_blk - 1 - lax.rem(p + dp + n_blk, n_blk), (1 - hh) * 2 + cc)

    step = block // CHUNKS

    def part(ref, i):
        return ref.at[pl.ds(i * step, step)]

    sems = [0]

    def flow(count):
        base = sems[0]
        sems[0] += count
        return base

    def copy(src, dst, k, device, ks=None):
        return pltpu.make_async_remote_copy(
            src_ref=src, dst_ref=dst, send_sem=ssem.at[k if ks is None else ks], recv_sem=rsem.at[k],
            device_id=device, device_id_type=MESH)

    f_own = flow(1)
    f_cross, f_crossf, f_prev, f_prevf = flow(CHUNKS), flow(CHUNKS), flow(CHUNKS), flow(CHUNKS)
    f_xprev, f_xprevf, f_nxt, f_nxt2, f_relay = flow(CHUNKS), flow(CHUNKS), flow(CHUNKS), flow(CHUNKS), flow(CHUNKS)
    f_gain = flow(10)
    f_far = flow(CHUNKS)

    core = dev(0, h, 1 - c)
    parts = range(CHUNKS)
    own_copy = copy(x, rows.at[OWN + c], f_own, core)
    cross = [copy(part(x, i), part(rows.at[CROSS + c], i), f_cross + i, dev(0, 1 - h, c)) for i in parts]
    crossf = [copy(part(rows.at[CROSS + c], i), part(rows.at[CROSS + c], i), f_crossf + i, core) for i in parts]
    prev = [copy(part(x, i), part(rows.at[PREV + c], i), f_prev + i, dev(1, h, c)) for i in parts]
    prev_relay = [copy(part(rows.at[CROSS + c], i), part(rows.at[PREV + c], i), f_prev + i, dev(1, 0, c)) for i in parts]
    prevf = [copy(part(rows.at[PREV + c], i), part(rows.at[PREV + c], i), f_prevf + i, core) for i in parts]
    xprev = [copy(part(rows.at[PREV + c], i), part(rows.at[XPREV + c], i), f_xprev + i, dev(0, 1 - h, c)) for i in parts]
    xprev_own = [copy(part(x, i), part(rows.at[XPREV + c], i), f_xprev + i, dev(1, 0, c)) for i in parts]
    xprevf = [copy(part(rows.at[XPREV + c], i), part(rows.at[XPREV + c], i), f_xprevf + i, core) for i in parts]
    nxtc = [copy(part(x, i), part(nxt, i), f_nxt + i, dev(-2, h, c)) for i in parts]
    to_relay = [copy(part(rows.at[CROSS + c], i), part(relay, i), f_relay + i, dev(-PERIOD, 1, c)) for i in parts[:NXT_CUT]]
    nxt_relay = [copy(part(relay, i), part(nxt, i), f_nxt + i, dev(PERIOD - 2, 1, c)) for i in parts[:NXT_CUT]]
    to_far = [copy(part(x, i), part(relay, i), f_relay + i, dev(ROW, 0, c)) for i in parts]
    far = [copy(part(relay, i), part(rows.at[XPREV + c], i), f_xprev + i, dev(1 - ROW, 0, c), f_far + i) for i in parts]
    nxt2_relay = [copy(part(nxt, i), part(nxt2, i), f_nxt2 + i, dev(0, 0, c)) for i in parts]
    nxt2c = [copy(part(x, i), part(nxt2, i), f_nxt2 + i, dev(-2, 1 - h, c)) for i in parts]

    local = pltpu.make_async_copy(x, rows.at[OWN + c], lsem)
    local.start()

    barrier = pltpu.get_barrier_semaphore()

    def hello(device):
        pl.semaphore_signal(barrier, inc=1, device_id=device, device_id_type=MESH)

    hello(core)
    hello(dev(0, 1 - h, c))
    pl.when(has_prev)(lambda: hello(dev(-1, h, c)))
    pl.when(has_nxt)(lambda: hello(dev(2, h, c)))

    @pl.when(first_a)
    def _():
        hello(dev(-1, 1, c))
        hello(dev(ROW - 1, 0, c))

    @pl.when(high_b)
    def _():
        hello(dev(2, 0, c))
        hello(dev(2 - PERIOD, 1, c))

    pl.when(turn_a)(lambda: hello(dev(-ROW, 1, c)))
    pl.when(low_b)(lambda: hello(dev(PERIOD, 0, c)))

    def one(flag):
        return jnp.where(flag, 1, 0)

    targets = 4 + one(last_b) + one(turn_a) + one(low)
    pl.semaphore_wait(barrier, targets)

    def sends_prev(i):
        return not_last if i < PREV_CUT else jnp.logical_or(not_last, is_a)

    def sends_nxt(i):
        return not_low if i < NXT_CUT else jnp.logical_or(not_low, is_b)

    for i in parts:
        cross[i].start()
        pl.when(sends_prev(i))(prev[i].start)
        pl.when(sends_nxt(i))(nxtc[i].start)
        pl.when(last_b)(xprev_own[i].start if i < XPREV_CUT else to_far[i].start)
        pl.when(low_a)(nxt2c[i].start)
        if i == 0:
            own_copy.start()

    rsum[...] = jnp.zeros_like(rsum)

    def squares(block_rows):
        v = block_rows.astype(jnp.float32)
        v = v * v
        total = v[:, 0:128]
        for k in range(1, width // 128):
            total = total + v[:, k * 128:(k + 1) * 128]
        return total

    def flat(acc):
        return jnp.sum(acc.T.reshape(16, 8, block), axis=0)

    def norms(s):
        total = jnp.sum(flat(squares(rows[s])), axis=0, keepdims=True) * SCALE
        rnorm[s] = jnp.broadcast_to(total, (8, block))

    def column_norms(block_rows):
        return jnp.sum(squares(block_rows), axis=1, keepdims=True) * SCALE

    def affinity(targets_, target_norms, s):
        products = lax.dot_general(targets_, rows[s], (((1,), (1,)), ((), ())), preferred_element_type=jnp.float32)
        return jnp.exp2(products * (2.0 * SCALE) - (target_norms + rnorm[s, 0:1, :]))

    def fold(e):
        total = e[:, 0:128]
        for k in range(1, block // 128):
            total = total + e[:, k * 128:(k + 1) * 128]
        return total

    def sweep(target, target_norms, slots, acc):
        for t in slots:
            e = affinity(target, target_norms, t)
            rsum[t] += jnp.sum(e.reshape(block // 8, 8, block), axis=0)
            acc = acc + fold(e)
        return acc

    def whole(ref, slots):
        target = ref[...]
        return flat(sweep(target, column_norms(target), slots, jnp.zeros((block, 128), jnp.float32)))

    local.wait()
    norms(OWN + c)

    def pass_relay(i):
        to_relay[i].wait_recv()
        nxt_relay[i].start()

    def pass_far(i):
        to_far[i].wait_recv()
        far[i].start()

    def pass_prev(i):
        prev[i].wait_recv()
        prevf[i].start()

    def pass_both(i):
        pass_prev(i)
        xprev[i].start()

    for i in parts:
        cross[i].wait_recv()
        if i < NXT_CUT:
            pl.when(low_a)(to_relay[i].start)
        if i < PREV_CUT:
            pl.when(last_b)(prev_relay[i].start)
        crossf[i].start()
        pl.when(inner)(functools.partial(pass_both, i))
        if 1 <= i <= NXT_CUT:
            pl.when(low_b)(functools.partial(pass_relay, i - 1))
        if i >= XPREV_CUT:
            pl.when(turn_a)(functools.partial(pass_far, i))

    own_copy.wait_recv()
    norms(OWN + 1 - c)
    for i in parts:
        crossf[i].wait_recv()
    norms(CROSS)
    norms(CROSS + 1)

    mine = rows[OWN + c]
    mine_norms = column_norms(mine)
    diagonal = lax.broadcasted_iota(jnp.int32, (block, block), 0) == lax.broadcasted_iota(jnp.int32, (block, block), 1)

    acc = jnp.zeros((block, 128), jnp.float32)
    for t in range(4):
        e = affinity(mine, mine_norms, t)
        if t < 2:
            e = jnp.where(jnp.logical_and(diagonal, c == t), 0.0, e)
        acc = acc + fold(e)
    rsum[OWN + c] += flat(acc)

    def get_prev():
        for i in parts:
            prevf[i].wait_recv()
        norms(PREV)
        norms(PREV + 1)

    def pass_xprev(some):
        for i in some:
            xprev[i].wait_recv()
            xprevf[i].start()

    def get_xprev():
        for i in parts:
            xprevf[i].wait_recv()
        norms(XPREV)
        norms(XPREV + 1)

    def get_nxt():
        for i in parts:
            nxtc[i].wait_recv()
        target = nxt[...]
        return target, column_norms(target), jnp.zeros((block, 128), jnp.float32)

    @pl.when(inner)
    def _():
        get_prev()

        @pl.when(jnp.logical_not(high_b))
        def _():
            rsum[PREV + c] += whole(rows.at[PREV + c], range(4))

    @pl.when(jnp.logical_and(inner, jnp.logical_not(high)))
    def _():
        pass_xprev(parts[:-1])
        target, target_norms, acc = get_nxt()
        acc = sweep(target, target_norms, range(4), acc)
        pass_xprev(parts[-1:])
        acc = sweep(target, target_norms, range(4, 6), acc)
        get_xprev()
        ncol[...] = flat(sweep(target, target_norms, range(6, 8), acc))

    @pl.when(first_b)
    def _():
        for i in parts:
            nxtc[i].wait_recv()
            nxt2_relay[i].start()
        ncol[...] = whole(nxt, range(4))

    def gain(src, slot, device, ks):
        return copy(src, gains.at[slot], f_gain + slot, device, f_gain + ks)

    g_own = [gain(rsum.at[OWN + 1 - c], 0, core, 0)]
    g_own += [gain(rsum.at[CROSS + k], 1 + c, dev(0, 1 - h, k), 1 + k) for k in range(2)]
    g_prev = [gain(rsum.at[PREV + k], 3 + c, dev(-1, h, k), 3 + k) for k in range(2)]
    g_xprev = [gain(rsum.at[XPREV + k], 5 + c, dev(-1, 1 - h, k), 5 + k) for k in range(2)]
    g_nxt = gain(ncol, 7, dev(2, h, c), 7)
    g_nxt2 = gain(ncol2, 8, dev(2, 1 - h, c), 8)

    @pl.when(first_a)
    def _():
        for i in parts[:-1]:
            pass_xprev([i])
            pass_prev(i)
        target, target_norms, acc = get_nxt()
        acc = sweep(target, target_norms, range(4), acc)
        other = rows[CROSS + c]
        other_norms = column_norms(other)
        for i in parts:
            nxt2c[i].wait_recv()
        target2 = nxt2[...]
        target2_norms = column_norms(target2)
        pass_xprev(parts[-1:])
        pass_prev(parts[-1])
        zero = jnp.zeros((block, 128), jnp.float32)
        accs = [zero, zero, acc, zero]

        def against(slots):
            for t in slots:
                accs[0] = sweep(mine, mine_norms, [t], accs[0])
                accs[1] = sweep(other, other_norms, [t], accs[1])
                accs[2] = sweep(target, target_norms, [t], accs[2])
                accs[3] = sweep(target2, target2_norms, [t], accs[3])

        get_xprev()
        against(range(XPREV, XPREV + 2))
        for q in g_xprev:
            q.start()
        get_prev()
        against(range(PREV, PREV + 2))
        for q in g_prev:
            q.start()
        rsum[OWN + c] += flat(accs[0])
        rsum[CROSS + c] += flat(accs[1])
        ncol[...] = flat(accs[2])
        ncol2[...] = flat(accs[3])

    @pl.when(high_a)
    def _():
        pass_xprev(parts)
        get_xprev()
        rsum[XPREV + c] += whole(rows.at[XPREV + c], range(4))

    @pl.when(high_b)
    def _():
        pass_xprev(parts)
        get_xprev()
        for i in parts:
            nxt2c[i].wait_recv()
        ncol2[...] = whole(nxt2, range(8))
        target, target_norms, acc = get_nxt()
        ncol[...] = flat(sweep(target, target_norms, range(8), acc))

    @pl.when(inner)
    def _():
        for q in g_xprev + g_prev:
            q.start()

    for q in g_own:
        q.start()

    pl.when(has_nxt)(g_nxt.start)
    pl.when(has_nxt2)(g_nxt2.start)

    def arrive(slot):
        copy(gains.at[slot], gains.at[slot], f_gain + slot, core).wait_recv()
        rsum[OWN + c] += gains[slot]

    for slot in range(3):
        arrive(slot)

    @pl.when(jnp.logical_or(not_last, is_a))
    def _():
        arrive(3)
        arrive(4)

    @pl.when(jnp.logical_or(not_last, is_b))
    def _():
        arrive(5)
        arrive(6)

    pl.when(jnp.logical_not(low_a))(lambda: arrive(7))
    pl.when(jnp.logical_or(low_a, second_b))(lambda: arrive(8))

    out[...] = jnp.log1p(jnp.sum(rsum[OWN + c], axis=0, keepdims=True))

    own_copy.wait_send()
    for i in parts:
        cross[i].wait_send()
        crossf[i].wait_send()
        pl.when(has_prev)(prevf[i].wait_send)
        pl.when(has_prev)(xprevf[i].wait_send)
        pl.when(inner)(xprev[i].wait_send)
        pl.when(low_a)(nxt2c[i].wait_send)
        pl.when(first_b)(nxt2_relay[i].wait_send)
        pl.when(sends_prev(i))(prev[i].wait_send)
        pl.when(sends_nxt(i))(nxtc[i].wait_send)
        if i < PREV_CUT:
            pl.when(last_b)(prev_relay[i].wait_send)
        if i < XPREV_CUT:
            pl.when(last_b)(xprev_own[i].wait_send)
        else:
            pl.when(last_b)(to_far[i].wait_send)
            pl.when(turn_a)(far[i].wait_send)
        if i < NXT_CUT:
            pl.when(low_b)(nxt_relay[i].wait_send)
            pl.when(low_a)(to_relay[i].wait_send)
    for q in g_own:
        q.wait_send()

    @pl.when(has_prev)
    def _():
        for q in g_xprev + g_prev:
            q.wait_send()

    pl.when(has_nxt)(g_nxt.wait_send)
    pl.when(has_nxt2)(g_nxt2.wait_send)


def solution(mesh):
    n_blk = mesh.shape["blk"]

    def body(embeddings):
        block, width = embeddings.shape
        n_sem = 1 + 10 * CHUNKS + 10
        sums = pl.pallas_call(
            functools.partial(kernel, n_blk, block, width),
            out_shape=jax.ShapeDtypeStruct((1, block), jnp.float32),
            in_specs=[pl.BlockSpec(memory_space=pl.ANY)],
            out_specs=pl.BlockSpec(memory_space=pltpu.VMEM),
            scratch_shapes=[
                pltpu.VMEM((8, block, width), jnp.bfloat16),
                pltpu.VMEM((block, width), jnp.bfloat16),
                pltpu.VMEM((block, width), jnp.bfloat16),
                pltpu.VMEM((block, width), jnp.bfloat16),
                pltpu.VMEM((8, 8, block), jnp.float32),
                pltpu.VMEM((8, 8, block), jnp.float32),
                pltpu.VMEM((8, block), jnp.float32),
                pltpu.VMEM((8, block), jnp.float32),
                pltpu.VMEM((9, 8, block), jnp.float32),
                pltpu.SemaphoreType.DMA,
                pltpu.SemaphoreType.DMA((n_sem,)),
                pltpu.SemaphoreType.DMA((n_sem,)),
            ],
            compiler_params=pltpu.CompilerParams(
                collective_id=0, has_side_effects=True, vmem_limit_bytes=40 * 2**20
            ),
            cost_estimate=pl.CostEstimate(flops=2 * 16 * block * block * width, bytes_accessed=2 * block * width,
                                          transcendentals=16 * block * block),
        )(embeddings)
        return sums.reshape(block)

    return jax.shard_map(
        body, mesh=mesh, in_specs=(P(("blk", "grp"), None),), out_specs=P(("blk", "grp")), check_vma=False
    )
```

```python
import functools
import math

import jax
import jax.numpy as jnp
from jax import lax
from jax.experimental import pallas as pl
from jax.experimental.pallas import tpu as pltpu
from jax.sharding import PartitionSpec as P

MESH = pl.DeviceIdType.MESH
SHARPNESS = 4.0
LOG2E = math.log2(math.e)
SCALE = SHARPNESS * LOG2E
CHUNKS = 4
PREV_CUT, NXT_CUT, NXT2_CUT = 3, 2, 4
PERIOD = 32
ROW = 8

OWN, CROSS, PREV, XPREV = 0, 2, 4, 6


def kernel(n_blk, block, width, x, out, rows, nxt, nxt2, relay, rsum, rnorm, ncol, ncol2, gains, lsem, ssem, rsem):
    p = n_blk - 1 - lax.axis_index("blk")
    g = lax.axis_index("grp")
    h = 1 - g // 2
    c = lax.rem(g, 2)
    m = lax.rem(p, PERIOD)
    is_a, is_b = h == 0, h == 1
    first, low, last, high = m == 0, m < 2, m == PERIOD - 1, m >= PERIOD - 2
    has_prev = jnp.logical_not(jnp.logical_and(first, is_b))
    has_nxt = jnp.logical_not(jnp.logical_and(high, is_a))
    has_nxt2 = jnp.logical_or(jnp.logical_and(first, is_a), jnp.logical_and(high, is_b))
    not_last, not_low = jnp.logical_not(last), jnp.logical_not(low)
    turn_a = jnp.logical_and(m == ROW - 1, is_a)
    low_a, low_b = jnp.logical_and(low, is_a), jnp.logical_and(low, is_b)
    high_a, high_b = jnp.logical_and(high, is_a), jnp.logical_and(high, is_b)
    last_a, last_b = jnp.logical_and(last, is_a), jnp.logical_and(last, is_b)
    inner = jnp.logical_not(first)
    first_a = jnp.logical_and(first, is_a)
    first_b = jnp.logical_and(first, is_b)
    second_b = jnp.logical_and(m == 2, is_b)

    def dev(dp, hh, cc):
        return (n_blk - 1 - lax.rem(p + dp + n_blk, n_blk), (1 - hh) * 2 + cc)

    step = block // CHUNKS

    def part(ref, i):
        return ref.at[pl.ds(i * step, step)]

    sems = [0]

    def flow(count):
        base = sems[0]
        sems[0] += count
        return base

    def copy(src, dst, k, device, ks=None):
        return pltpu.make_async_remote_copy(
            src_ref=src, dst_ref=dst, send_sem=ssem.at[k if ks is None else ks], recv_sem=rsem.at[k],
            device_id=device, device_id_type=MESH)

    f_own = flow(1)
    f_cross, f_crossf, f_prev, f_prevf = flow(CHUNKS), flow(CHUNKS), flow(CHUNKS), flow(CHUNKS)
    f_xprev, f_xprevf, f_nxt, f_nxt2, f_relay = flow(CHUNKS), flow(CHUNKS), flow(CHUNKS), flow(CHUNKS), flow(CHUNKS)
    f_gain = flow(10)
    f_far = flow(CHUNKS)

    core = dev(0, h, 1 - c)
    parts = range(CHUNKS)
    own_copy = copy(x, rows.at[OWN + c], f_own, core)
    cross = [copy(part(x, i), part(rows.at[CROSS + c], i), f_cross + i, dev(0, 1 - h, c)) for i in parts]
    crossf = [copy(part(rows.at[CROSS + c], i), part(rows.at[CROSS + c], i), f_crossf + i, core) for i in parts]
    prev = [copy(part(x, i), part(rows.at[PREV + c], i), f_prev + i, dev(1, h, c)) for i in parts]
    prev_relay = [copy(part(rows.at[CROSS + c], i), part(rows.at[PREV + c], i), f_prev + i, dev(1, 0, c)) for i in parts]
    prevf = [copy(part(rows.at[PREV + c], i), part(rows.at[PREV + c], i), f_prevf + i, core) for i in parts]
    xprev = [copy(part(rows.at[PREV + c], i), part(rows.at[XPREV + c], i), f_xprev + i, dev(0, 1 - h, c)) for i in parts]
    xprev_own = [copy(part(x, i), part(rows.at[XPREV + c], i), f_xprev + i, dev(1, 0, c)) for i in parts]
    xprevf = [copy(part(rows.at[XPREV + c], i), part(rows.at[XPREV + c], i), f_xprevf + i, core) for i in parts]
    nxtc = [copy(part(x, i), part(nxt, i), f_nxt + i, dev(-2, h, c)) for i in parts]
    to_relay = [copy(part(rows.at[CROSS + c], i), part(relay, i), f_relay + i, dev(-PERIOD, 1, c)) for i in parts[:NXT_CUT]]
    nxt_relay = [copy(part(relay, i), part(nxt, i), f_nxt + i, dev(PERIOD - 2, 1, c)) for i in parts[:NXT_CUT]]
    to_far = [copy(part(x, i), part(relay, i), f_relay + i, dev(ROW, 0, c)) for i in parts]
    far = [copy(part(relay, i), part(rows.at[XPREV + c], i), f_xprev + i, dev(1 - ROW, 0, c), f_far + i) for i in parts]
    to_far_prev = [copy(part(rows.at[CROSS + c], i), part(relay, i - PREV_CUT), f_relay + i - PREV_CUT, dev(ROW, 0, c))
                   if i >= PREV_CUT else None for i in parts]
    far_prev = [copy(part(relay, i - PREV_CUT), part(rows.at[PREV + c], i), f_prev + i, dev(1 - ROW, 0, c), f_far + i - PREV_CUT)
                if i >= PREV_CUT else None for i in parts]
    nxt2_relay = [copy(part(nxt, i), part(nxt2, i), f_nxt2 + i, dev(0, 0, c)) for i in parts]
    nxt2_cross = [copy(part(rows.at[CROSS + c], i), part(nxt2, i), f_nxt2 + i, dev(-2, 1, c)) for i in parts]
    nxt2c = [copy(part(x, i), part(nxt2, i), f_nxt2 + i, dev(-2, 1 - h, c)) for i in parts]

    local = pltpu.make_async_copy(x, rows.at[OWN + c], lsem)
    local.start()

    barrier = pltpu.get_barrier_semaphore()

    def hello(device):
        pl.semaphore_signal(barrier, inc=1, device_id=device, device_id_type=MESH)

    hello(core)
    hello(dev(0, 1 - h, c))
    pl.when(inner)(lambda: hello(dev(-1, h, c)))
    pl.when(has_nxt)(lambda: hello(dev(2, h, c)))

    @pl.when(first_a)
    def _():
        hello(dev(-1, 1, c))
        hello(dev(ROW - 1, 0, c))

    @pl.when(high_b)
    def _():
        hello(dev(2, 0, c))
        hello(dev(2 - PERIOD, 1, c))

    pl.when(turn_a)(lambda: hello(dev(-ROW, 1, c)))
    pl.when(low_b)(lambda: hello(dev(PERIOD, 0, c)))

    def one(flag):
        return jnp.where(flag, 1, 0)

    targets = 3 + one(not_last) + 2 * one(last_b) + one(turn_a) + one(low)
    pl.semaphore_wait(barrier, targets)

    def sends_nxt(i):
        return not_low if i < NXT_CUT else jnp.logical_or(not_low, is_b)

    for i in parts:
        cross[i].start()
        pl.when(not_last)(prev[i].start)
        pl.when(sends_nxt(i))(nxtc[i].start)
        pl.when(last_b)(xprev_own[i].start if i < PREV_CUT else to_far[i].start)
        if i < NXT2_CUT:
            pl.when(low_a)(nxt2c[i].start)
        if i == 0:
            own_copy.start()

    rsum[...] = jnp.zeros_like(rsum)

    def squares(block_rows):
        v = block_rows.astype(jnp.float32)
        v = v * v
        total = v[:, 0:128]
        for k in range(1, width // 128):
            total = total + v[:, k * 128:(k + 1) * 128]
        return total

    def flat(acc):
        return jnp.sum(acc.T.reshape(16, 8, block), axis=0)

    def norms(s):
        total = jnp.sum(flat(squares(rows[s])), axis=0, keepdims=True) * SCALE
        rnorm[s] = jnp.broadcast_to(total, (8, block))

    def column_norms(block_rows):
        return jnp.sum(squares(block_rows), axis=1, keepdims=True) * SCALE

    def affinity(targets_, target_norms, s):
        products = lax.dot_general(targets_, rows[s], (((1,), (1,)), ((), ())), preferred_element_type=jnp.float32)
        return jnp.exp2(products * (2.0 * SCALE) - (target_norms + rnorm[s, 0:1, :]))

    def fold(e):
        total = e[:, 0:128]
        for k in range(1, block // 128):
            total = total + e[:, k * 128:(k + 1) * 128]
        return total

    def sweep(target, target_norms, slots, acc):
        for t in slots:
            e = affinity(target, target_norms, t)
            rsum[t] += jnp.sum(e.reshape(block // 8, 8, block), axis=0)
            acc = acc + fold(e)
        return acc

    def whole(ref, slots):
        target = ref[...]
        return flat(sweep(target, column_norms(target), slots, jnp.zeros((block, 128), jnp.float32)))

    local.wait()
    norms(OWN + c)

    def pass_relay(i):
        to_relay[i].wait_recv()
        nxt_relay[i].start()

    def pass_far(i):
        to_far[i].wait_recv()
        far[i].start()
        to_far_prev[i].wait_recv()
        far_prev[i].start()

    def pass_prev(i):
        prev[i].wait_recv()
        prevf[i].start()

    def pass_both(i):
        pass_prev(i)
        xprev[i].start()

    @pl.when(last_a)
    def _():
        for i in parts:
            pass_both(i)

    for i in parts:
        cross[i].wait_recv()
        if i < NXT_CUT:
            pl.when(low_a)(to_relay[i].start)
        if i >= NXT2_CUT:
            pl.when(low_b)(nxt2_cross[i].start)
        pl.when(last_b)(prev_relay[i].start if i < PREV_CUT else to_far_prev[i].start)
        crossf[i].start()
        pl.when(jnp.logical_and(inner, jnp.logical_not(last_a)))(functools.partial(pass_both, i))
        if 1 <= i <= NXT_CUT:
            pl.when(low_b)(functools.partial(pass_relay, i - 1))
        if i >= PREV_CUT:
            pl.when(turn_a)(functools.partial(pass_far, i))

    own_copy.wait_recv()
    norms(OWN + 1 - c)
    for i in parts:
        crossf[i].wait_recv()
    norms(CROSS)
    norms(CROSS + 1)

    mine = rows[OWN + c]
    mine_norms = column_norms(mine)
    diagonal = lax.broadcasted_iota(jnp.int32, (block, block), 0) == lax.broadcasted_iota(jnp.int32, (block, block), 1)

    acc = jnp.zeros((block, 128), jnp.float32)
    for t in range(4):
        e = affinity(mine, mine_norms, t)
        if t < 2:
            e = jnp.where(jnp.logical_and(diagonal, c == t), 0.0, e)
        acc = acc + fold(e)
    rsum[OWN + c] += flat(acc)

    def get_prev():
        for i in parts:
            prevf[i].wait_recv()
        norms(PREV)
        norms(PREV + 1)

    def pass_xprev(some):
        for i in some:
            xprev[i].wait_recv()
            xprevf[i].start()

    def get_xprev():
        for i in parts:
            xprevf[i].wait_recv()
        norms(XPREV)
        norms(XPREV + 1)

    def get_nxt():
        for i in parts:
            nxtc[i].wait_recv()
        target = nxt[...]
        return target, column_norms(target), jnp.zeros((block, 128), jnp.float32)

    @pl.when(inner)
    def _():
        get_prev()

        @pl.when(jnp.logical_not(high_b))
        def _():
            rsum[PREV + c] += whole(rows.at[PREV + c], range(4))

    @pl.when(jnp.logical_and(inner, jnp.logical_not(high)))
    def _():
        pass_xprev(parts[:-1])
        target, target_norms, acc = get_nxt()
        acc = sweep(target, target_norms, range(4), acc)
        pass_xprev(parts[-1:])
        acc = sweep(target, target_norms, range(4, 6), acc)
        get_xprev()
        ncol[...] = flat(sweep(target, target_norms, range(6, 8), acc))

    @pl.when(first_b)
    def _():
        for i in parts:
            nxtc[i].wait_recv()
            nxt2_relay[i].start()
        ncol[...] = whole(nxt, range(4))

    def gain(src, slot, device, ks):
        return copy(src, gains.at[slot], f_gain + slot, device, f_gain + ks)

    g_own = [gain(rsum.at[OWN + 1 - c], 0, core, 0)]
    g_own += [gain(rsum.at[CROSS + k], 1 + c, dev(0, 1 - h, k), 1 + k) for k in range(2)]
    g_prev = [gain(rsum.at[PREV + k], 3 + c, dev(-1, h, k), 3 + k) for k in range(2)]
    g_xprev = [gain(rsum.at[XPREV + k], 5 + c, dev(-1, 1 - h, k), 5 + k) for k in range(2)]
    g_nxt = gain(ncol, 7, dev(2, h, c), 7)
    g_nxt2 = gain(ncol2, 8, dev(2, 1 - h, c), 8)

    @pl.when(first_a)
    def _():
        for i in parts[:-1]:
            pass_xprev([i])
            pass_prev(i)
        other = rows[CROSS + c]
        other_norms = column_norms(other)
        pass_xprev(parts[-1:])
        pass_prev(parts[-1])
        zero = jnp.zeros((block, 128), jnp.float32)
        mine_acc, other_acc = zero, zero
        get_xprev()
        mine_acc = sweep(mine, mine_norms, range(XPREV, 8), mine_acc)
        other_acc = sweep(other, other_norms, range(XPREV, 8), other_acc)
        get_prev()
        mine_acc = sweep(mine, mine_norms, range(PREV, XPREV), mine_acc)
        other_acc = sweep(other, other_norms, range(PREV, XPREV), other_acc)
        target, target_norms, acc = get_nxt()
        acc = sweep(target, target_norms, range(PREV, 8), acc)
        for i in parts:
            nxt2c[i].wait_recv()
        target2 = nxt2[...]
        acc2 = sweep(target2, column_norms(target2), range(PREV, 8), zero)
        for q in g_xprev:
            q.start()
        for q in g_prev:
            q.start()
        rsum[OWN + c] += flat(mine_acc)
        rsum[CROSS + c] += flat(other_acc)
        ncol[...] = flat(sweep(target, target_norms, range(4), acc))
        ncol2[...] = flat(acc2)

    @pl.when(high_a)
    def _():
        pass_xprev(parts)
        get_xprev()
        rsum[XPREV + c] += whole(rows.at[XPREV + c], range(4))

    @pl.when(high_b)
    def _():
        pass_xprev(parts)
        for i in parts:
            nxt2c[i].wait_recv()
        target2 = nxt2[...]
        target2_norms = column_norms(target2)
        acc2 = sweep(target2, target2_norms, range(XPREV), jnp.zeros((block, 128), jnp.float32))
        target, target_norms, acc = get_nxt()
        acc = sweep(target, target_norms, range(XPREV), acc)
        get_xprev()
        ncol2[...] = flat(sweep(target2, target2_norms, range(XPREV, 8), acc2))
        ncol[...] = flat(sweep(target, target_norms, range(XPREV, 8), acc))

    @pl.when(inner)
    def _():
        for q in g_xprev + g_prev:
            q.start()

    for q in g_own:
        q.start()

    pl.when(has_nxt)(g_nxt.start)
    pl.when(has_nxt2)(g_nxt2.start)

    def arrive(slot):
        copy(gains.at[slot], gains.at[slot], f_gain + slot, core).wait_recv()
        rsum[OWN + c] += gains[slot]

    for slot in range(3):
        arrive(slot)

    @pl.when(jnp.logical_or(not_last, is_a))
    def _():
        arrive(3)
        arrive(4)

    @pl.when(jnp.logical_or(not_last, is_b))
    def _():
        arrive(5)
        arrive(6)

    pl.when(jnp.logical_not(low_a))(lambda: arrive(7))
    pl.when(jnp.logical_or(low_a, second_b))(lambda: arrive(8))

    out[...] = jnp.log1p(jnp.sum(rsum[OWN + c], axis=0, keepdims=True))

    own_copy.wait_send()
    for i in parts:
        cross[i].wait_send()
        crossf[i].wait_send()
        pl.when(has_prev)(prevf[i].wait_send)
        pl.when(has_prev)(xprevf[i].wait_send)
        pl.when(inner)(xprev[i].wait_send)
        if i < NXT2_CUT:
            pl.when(low_a)(nxt2c[i].wait_send)
        else:
            pl.when(low_b)(nxt2_cross[i].wait_send)
        pl.when(first_b)(nxt2_relay[i].wait_send)
        pl.when(not_last)(prev[i].wait_send)
        pl.when(sends_nxt(i))(nxtc[i].wait_send)
        if i < PREV_CUT:
            pl.when(last_b)(prev_relay[i].wait_send)
            pl.when(last_b)(xprev_own[i].wait_send)
        else:
            pl.when(last_b)(to_far[i].wait_send)
            pl.when(last_b)(to_far_prev[i].wait_send)
            pl.when(turn_a)(far[i].wait_send)
            pl.when(turn_a)(far_prev[i].wait_send)
        if i < NXT_CUT:
            pl.when(low_b)(nxt_relay[i].wait_send)
            pl.when(low_a)(to_relay[i].wait_send)
    for q in g_own:
        q.wait_send()

    @pl.when(has_prev)
    def _():
        for q in g_xprev + g_prev:
            q.wait_send()

    pl.when(has_nxt)(g_nxt.wait_send)
    pl.when(has_nxt2)(g_nxt2.wait_send)


def solution(mesh):
    n_blk = mesh.shape["blk"]

    def body(embeddings):
        block, width = embeddings.shape
        n_sem = 1 + 10 * CHUNKS + 10
        sums = pl.pallas_call(
            functools.partial(kernel, n_blk, block, width),
            out_shape=jax.ShapeDtypeStruct((1, block), jnp.float32),
            in_specs=[pl.BlockSpec(memory_space=pl.ANY)],
            out_specs=pl.BlockSpec(memory_space=pltpu.VMEM),
            scratch_shapes=[
                pltpu.VMEM((8, block, width), jnp.bfloat16),
                pltpu.VMEM((block, width), jnp.bfloat16),
                pltpu.VMEM((block, width), jnp.bfloat16),
                pltpu.VMEM((block, width), jnp.bfloat16),
                pltpu.VMEM((8, 8, block), jnp.float32),
                pltpu.VMEM((8, 8, block), jnp.float32),
                pltpu.VMEM((8, block), jnp.float32),
                pltpu.VMEM((8, block), jnp.float32),
                pltpu.VMEM((9, 8, block), jnp.float32),
                pltpu.SemaphoreType.DMA,
                pltpu.SemaphoreType.DMA((n_sem,)),
                pltpu.SemaphoreType.DMA((n_sem,)),
            ],
            compiler_params=pltpu.CompilerParams(
                collective_id=0, has_side_effects=True, vmem_limit_bytes=40 * 2**20
            ),
            cost_estimate=pl.CostEstimate(flops=2 * 16 * block * block * width, bytes_accessed=2 * block * width,
                                          transcendentals=16 * block * block),
        )(embeddings)
        return sums.reshape(block)

    return jax.shard_map(
        body, mesh=mesh, in_specs=(P(("blk", "grp"), None),), out_specs=P(("blk", "grp")), check_vma=False
    )
```

```python
import functools
import math

import jax
import jax.numpy as jnp
from jax import lax
from jax.experimental import pallas as pl
from jax.experimental.pallas import tpu as pltpu
from jax.sharding import PartitionSpec as P

MESH = pl.DeviceIdType.MESH
SHARPNESS = 4.0
LOG2E = math.log2(math.e)
SCALE = SHARPNESS * LOG2E
CHUNKS = 4
PREV_CUT, NXT_CUT, NXT2_CUT = 3, 2, 4
PERIOD = 32
ROW = 8

OWN, CROSS, PREV, XPREV = 0, 2, 4, 6


def kernel(n_blk, block, width, x, out, rows, nxt, nxt2, relay, rsum, rnorm, ncol, ncol2, gains, lsem, ssem, rsem):
    p = n_blk - 1 - lax.axis_index("blk")
    g = lax.axis_index("grp")
    h = 1 - g // 2
    c = lax.rem(g, 2)
    m = lax.rem(p, PERIOD)
    is_a, is_b = h == 0, h == 1
    first, low, last, high = m == 0, m < 2, m == PERIOD - 1, m >= PERIOD - 2
    has_prev = jnp.logical_not(jnp.logical_and(first, is_b))
    has_nxt = jnp.logical_not(jnp.logical_and(high, is_a))
    has_nxt2 = jnp.logical_or(jnp.logical_and(first, is_a), jnp.logical_and(high, is_b))
    not_last, not_low = jnp.logical_not(last), jnp.logical_not(low)
    turn_a = jnp.logical_and(m == ROW - 1, is_a)
    low_a, low_b = jnp.logical_and(low, is_a), jnp.logical_and(low, is_b)
    high_a, high_b = jnp.logical_and(high, is_a), jnp.logical_and(high, is_b)
    last_a, last_b = jnp.logical_and(last, is_a), jnp.logical_and(last, is_b)
    inner = jnp.logical_not(first)
    first_a = jnp.logical_and(first, is_a)
    first_b = jnp.logical_and(first, is_b)
    second_b = jnp.logical_and(m == 2, is_b)

    def dev(dp, hh, cc):
        return (n_blk - 1 - lax.rem(p + dp + n_blk, n_blk), (1 - hh) * 2 + cc)

    step = block // CHUNKS

    def part(ref, i):
        return ref.at[pl.ds(i * step, step)]

    sems = [0]

    def flow(count):
        base = sems[0]
        sems[0] += count
        return base

    def copy(src, dst, k, device, ks=None):
        return pltpu.make_async_remote_copy(
            src_ref=src, dst_ref=dst, send_sem=ssem.at[k if ks is None else ks], recv_sem=rsem.at[k],
            device_id=device, device_id_type=MESH)

    f_own = flow(1)
    f_cross, f_crossf, f_prev, f_prevf = flow(CHUNKS), flow(CHUNKS), flow(CHUNKS), flow(CHUNKS)
    f_xprev, f_xprevf, f_nxt, f_nxt2, f_relay = flow(CHUNKS), flow(CHUNKS), flow(CHUNKS), flow(CHUNKS), flow(CHUNKS)
    f_gain = flow(10)
    f_far = flow(CHUNKS)

    core = dev(0, h, 1 - c)
    parts = range(CHUNKS)
    own_copy = copy(x, rows.at[OWN + c], f_own, core)
    cross = [copy(part(x, i), part(rows.at[CROSS + c], i), f_cross + i, dev(0, 1 - h, c)) for i in parts]
    crossf = [copy(part(rows.at[CROSS + c], i), part(rows.at[CROSS + c], i), f_crossf + i, core) for i in parts]
    prev = [copy(part(x, i), part(rows.at[PREV + c], i), f_prev + i, dev(1, h, c)) for i in parts]
    prev_relay = [copy(part(rows.at[CROSS + c], i), part(rows.at[PREV + c], i), f_prev + i, dev(1, 0, c)) for i in parts]
    prevf = [copy(part(rows.at[PREV + c], i), part(rows.at[PREV + c], i), f_prevf + i, core) for i in parts]
    xprev = [copy(part(rows.at[PREV + c], i), part(rows.at[XPREV + c], i), f_xprev + i, dev(0, 1 - h, c)) for i in parts]
    xprev_own = [copy(part(x, i), part(rows.at[XPREV + c], i), f_xprev + i, dev(1, 0, c)) for i in parts]
    xprevf = [copy(part(rows.at[XPREV + c], i), part(rows.at[XPREV + c], i), f_xprevf + i, core) for i in parts]
    nxtc = [copy(part(x, i), part(nxt, i), f_nxt + i, dev(-2, h, c)) for i in parts]
    to_relay = [copy(part(rows.at[CROSS + c], i), part(relay, i), f_relay + i, dev(-PERIOD, 1, c)) for i in parts[:NXT_CUT]]
    nxt_relay = [copy(part(relay, i), part(nxt, i), f_nxt + i, dev(PERIOD - 2, 1, c)) for i in parts[:NXT_CUT]]
    to_far = [copy(part(x, i), part(relay, i), f_relay + i, dev(ROW, 0, c)) for i in parts]
    far = [copy(part(relay, i), part(rows.at[XPREV + c], i), f_xprev + i, dev(1 - ROW, 0, c), f_far + i) for i in parts]
    to_far_prev = [copy(part(rows.at[CROSS + c], i), part(relay, i - PREV_CUT), f_relay + i - PREV_CUT, dev(ROW, 0, c))
                   if i >= PREV_CUT else None for i in parts]
    far_prev = [copy(part(relay, i - PREV_CUT), part(rows.at[PREV + c], i), f_prev + i, dev(1 - ROW, 0, c), f_far + i - PREV_CUT)
                if i >= PREV_CUT else None for i in parts]
    nxt2_relay = [copy(part(nxt, i), part(nxt2, i), f_nxt2 + i, dev(0, 0, c)) for i in parts]
    nxt2_cross = [copy(part(rows.at[CROSS + c], i), part(nxt2, i), f_nxt2 + i, dev(-2, 1, c)) for i in parts]
    nxt2c = [copy(part(x, i), part(nxt2, i), f_nxt2 + i, dev(-2, 1 - h, c)) for i in parts]

    local = pltpu.make_async_copy(x, rows.at[OWN + c], lsem)
    local.start()

    barrier = pltpu.get_barrier_semaphore()

    def hello(device):
        pl.semaphore_signal(barrier, inc=1, device_id=device, device_id_type=MESH)

    hello(core)
    hello(dev(0, 1 - h, c))
    pl.when(inner)(lambda: hello(dev(-1, h, c)))
    pl.when(has_nxt)(lambda: hello(dev(2, h, c)))

    @pl.when(first_a)
    def _():
        hello(dev(-1, 1, c))
        hello(dev(ROW - 1, 0, c))

    @pl.when(high_b)
    def _():
        hello(dev(2, 0, c))
        hello(dev(2 - PERIOD, 1, c))

    pl.when(turn_a)(lambda: hello(dev(-ROW, 1, c)))
    pl.when(low_b)(lambda: hello(dev(PERIOD, 0, c)))

    def one(flag):
        return jnp.where(flag, 1, 0)

    targets = 3 + one(not_last) + 2 * one(last_b) + one(turn_a) + one(low)
    pl.semaphore_wait(barrier, targets)

    def sends_nxt(i):
        return not_low if i < NXT_CUT else jnp.logical_or(not_low, is_b)

    for i in parts:
        cross[i].start()
        pl.when(not_last)(prev[i].start)
        pl.when(sends_nxt(i))(nxtc[i].start)
        pl.when(last_b)(xprev_own[i].start if i < PREV_CUT else to_far[i].start)
        if i < NXT2_CUT:
            pl.when(low_a)(nxt2c[i].start)
        if i == 0:
            own_copy.start()

    rsum[...] = jnp.zeros_like(rsum)

    def squares(block_rows):
        v = block_rows.astype(jnp.float32)
        v = v * v
        total = v[:, 0:128]
        for k in range(1, width // 128):
            total = total + v[:, k * 128:(k + 1) * 128]
        return total

    def flat(acc):
        return jnp.sum(acc.T.reshape(16, 8, block), axis=0)

    def norms(s):
        total = jnp.sum(flat(squares(rows[s])), axis=0, keepdims=True) * SCALE
        rnorm[s] = jnp.broadcast_to(total, (8, block))

    def column_norms(block_rows):
        return jnp.sum(squares(block_rows), axis=1, keepdims=True) * SCALE

    def affinity(targets_, target_norms, s):
        products = lax.dot_general(targets_, rows[s], (((1,), (1,)), ((), ())), preferred_element_type=jnp.float32)
        return jnp.exp2(products * (2.0 * SCALE) - (target_norms + rnorm[s, 0:1, :]))

    def fold(e):
        total = e[:, 0:128]
        for k in range(1, block // 128):
            total = total + e[:, k * 128:(k + 1) * 128]
        return total

    def sweep(target, target_norms, slots, acc):
        for t in slots:
            e = affinity(target, target_norms, t)
            rsum[t] += jnp.sum(e.reshape(block // 8, 8, block), axis=0)
            acc = acc + fold(e)
        return acc

    def whole(ref, slots):
        target = ref[...]
        return flat(sweep(target, column_norms(target), slots, jnp.zeros((block, 128), jnp.float32)))

    local.wait()
    norms(OWN + c)

    def pass_relay(i):
        to_relay[i].wait_recv()
        nxt_relay[i].start()

    def pass_far(i):
        to_far[i].wait_recv()
        far[i].start()
        to_far_prev[i].wait_recv()
        far_prev[i].start()

    def pass_prev(i):
        prev[i].wait_recv()
        prevf[i].start()

    def pass_both(i):
        pass_prev(i)
        xprev[i].start()

    @pl.when(last_a)
    def _():
        for i in parts:
            pass_both(i)

    for i in parts:
        cross[i].wait_recv()
        if i < NXT_CUT:
            pl.when(low_a)(to_relay[i].start)
        if i >= NXT2_CUT:
            pl.when(low_b)(nxt2_cross[i].start)
        pl.when(last_b)(prev_relay[i].start if i < PREV_CUT else to_far_prev[i].start)
        crossf[i].start()
        pl.when(jnp.logical_and(inner, jnp.logical_not(last_a)))(functools.partial(pass_both, i))
        if 1 <= i <= NXT_CUT:
            pl.when(low_b)(functools.partial(pass_relay, i - 1))
        if i >= PREV_CUT:
            pl.when(turn_a)(functools.partial(pass_far, i))

    own_copy.wait_recv()
    norms(OWN + 1 - c)
    for i in parts:
        crossf[i].wait_recv()
    norms(CROSS)
    norms(CROSS + 1)

    mine = rows[OWN + c]
    mine_norms = column_norms(mine)
    diagonal = lax.broadcasted_iota(jnp.int32, (block, block), 0) == lax.broadcasted_iota(jnp.int32, (block, block), 1)

    acc = jnp.zeros((block, 128), jnp.float32)
    for t in range(4):
        e = affinity(mine, mine_norms, t)
        if t < 2:
            e = jnp.where(jnp.logical_and(diagonal, c == t), 0.0, e)
        acc = acc + fold(e)
    rsum[OWN + c] += flat(acc)

    def get_prev():
        for i in parts:
            prevf[i].wait_recv()
        norms(PREV)
        norms(PREV + 1)

    def pass_xprev(some):
        for i in some:
            xprev[i].wait_recv()
            xprevf[i].start()

    def get_xprev():
        for i in parts:
            xprevf[i].wait_recv()
        norms(XPREV)
        norms(XPREV + 1)

    def get_nxt():
        for i in parts:
            nxtc[i].wait_recv()
        target = nxt[...]
        return target, column_norms(target), jnp.zeros((block, 128), jnp.float32)

    @pl.when(inner)
    def _():
        get_prev()

        @pl.when(jnp.logical_not(high_b))
        def _():
            rsum[PREV + c] += whole(rows.at[PREV + c], range(4))

    @pl.when(jnp.logical_and(inner, jnp.logical_not(high)))
    def _():
        pass_xprev(parts[:-1])
        target, target_norms, acc = get_nxt()
        acc = sweep(target, target_norms, range(4), acc)
        pass_xprev(parts[-1:])
        acc = sweep(target, target_norms, range(4, 6), acc)
        get_xprev()
        ncol[...] = flat(sweep(target, target_norms, range(6, 8), acc))

    @pl.when(first_b)
    def _():
        for i in parts:
            nxtc[i].wait_recv()
            nxt2_relay[i].start()
        ncol[...] = whole(nxt, range(4))

    def gain(src, slot, device, ks):
        return copy(src, gains.at[slot], f_gain + slot, device, f_gain + ks)

    g_own = [gain(rsum.at[OWN + 1 - c], 0, core, 0)]
    g_own += [gain(rsum.at[CROSS + k], 1 + c, dev(0, 1 - h, k), 1 + k) for k in range(2)]
    g_prev = [gain(rsum.at[PREV + k], 3 + c, dev(-1, h, k), 3 + k) for k in range(2)]
    g_xprev = [gain(rsum.at[XPREV + k], 5 + c, dev(-1, 1 - h, k), 5 + k) for k in range(2)]
    g_nxt = gain(ncol, 7, dev(2, h, c), 7)
    g_nxt2 = gain(ncol2, 8, dev(2, 1 - h, c), 8)

    @pl.when(first_a)
    def _():
        for i in parts[:-1]:
            pass_xprev([i])
            pass_prev(i)
        other = rows[CROSS + c]
        other_norms = column_norms(other)
        pass_xprev(parts[-1:])
        pass_prev(parts[-1])
        zero = jnp.zeros((block, 128), jnp.float32)
        mine_acc, other_acc = zero, zero
        get_xprev()
        mine_acc = sweep(mine, mine_norms, range(XPREV, 8), mine_acc)
        other_acc = sweep(other, other_norms, range(XPREV, 8), other_acc)
        get_prev()
        mine_acc = sweep(mine, mine_norms, range(PREV, XPREV), mine_acc)
        other_acc = sweep(other, other_norms, range(PREV, XPREV), other_acc)
        target, target_norms, acc = get_nxt()
        acc = sweep(target, target_norms, range(XPREV, 8), acc)
        for i in parts:
            nxt2c[i].wait_recv()
        target2 = nxt2[...]
        target2_norms = column_norms(target2)
        acc2 = sweep(target2, target2_norms, range(XPREV, 8), zero)
        for q in g_xprev:
            q.start()
        acc = sweep(target, target_norms, range(PREV, XPREV), acc)
        acc2 = sweep(target2, target2_norms, range(PREV, XPREV), acc2)
        for q in g_prev:
            q.start()
        rsum[OWN + c] += flat(mine_acc)
        rsum[CROSS + c] += flat(other_acc)
        ncol[...] = flat(sweep(target, target_norms, range(4), acc))
        ncol2[...] = flat(acc2)

    @pl.when(high_a)
    def _():
        pass_xprev(parts)
        get_xprev()
        rsum[XPREV + c] += whole(rows.at[XPREV + c], range(4))

    @pl.when(high_b)
    def _():
        pass_xprev(parts)
        for i in parts:
            nxt2c[i].wait_recv()
        target2 = nxt2[...]
        target2_norms = column_norms(target2)
        acc2 = sweep(target2, target2_norms, range(XPREV), jnp.zeros((block, 128), jnp.float32))
        target, target_norms, acc = get_nxt()
        acc = sweep(target, target_norms, range(XPREV), acc)
        get_xprev()
        ncol2[...] = flat(sweep(target2, target2_norms, range(XPREV, 8), acc2))
        ncol[...] = flat(sweep(target, target_norms, range(XPREV, 8), acc))

    @pl.when(inner)
    def _():
        for q in g_xprev + g_prev:
            q.start()

    for q in g_own:
        q.start()

    pl.when(has_nxt)(g_nxt.start)
    pl.when(has_nxt2)(g_nxt2.start)

    def arrive(slot):
        copy(gains.at[slot], gains.at[slot], f_gain + slot, core).wait_recv()
        rsum[OWN + c] += gains[slot]

    for slot in range(3):
        arrive(slot)

    @pl.when(jnp.logical_or(not_last, is_a))
    def _():
        arrive(3)
        arrive(4)

    @pl.when(jnp.logical_or(not_last, is_b))
    def _():
        arrive(5)
        arrive(6)

    pl.when(jnp.logical_not(low_a))(lambda: arrive(7))
    pl.when(jnp.logical_or(low_a, second_b))(lambda: arrive(8))

    out[...] = jnp.log1p(jnp.sum(rsum[OWN + c], axis=0, keepdims=True))

    own_copy.wait_send()
    for i in parts:
        cross[i].wait_send()
        crossf[i].wait_send()
        pl.when(has_prev)(prevf[i].wait_send)
        pl.when(has_prev)(xprevf[i].wait_send)
        pl.when(inner)(xprev[i].wait_send)
        if i < NXT2_CUT:
            pl.when(low_a)(nxt2c[i].wait_send)
        else:
            pl.when(low_b)(nxt2_cross[i].wait_send)
        pl.when(first_b)(nxt2_relay[i].wait_send)
        pl.when(not_last)(prev[i].wait_send)
        pl.when(sends_nxt(i))(nxtc[i].wait_send)
        if i < PREV_CUT:
            pl.when(last_b)(prev_relay[i].wait_send)
            pl.when(last_b)(xprev_own[i].wait_send)
        else:
            pl.when(last_b)(to_far[i].wait_send)
            pl.when(last_b)(to_far_prev[i].wait_send)
            pl.when(turn_a)(far[i].wait_send)
            pl.when(turn_a)(far_prev[i].wait_send)
        if i < NXT_CUT:
            pl.when(low_b)(nxt_relay[i].wait_send)
            pl.when(low_a)(to_relay[i].wait_send)
    for q in g_own:
        q.wait_send()

    @pl.when(has_prev)
    def _():
        for q in g_xprev + g_prev:
            q.wait_send()

    pl.when(has_nxt)(g_nxt.wait_send)
    pl.when(has_nxt2)(g_nxt2.wait_send)


def solution(mesh):
    n_blk = mesh.shape["blk"]

    def body(embeddings):
        block, width = embeddings.shape
        n_sem = 1 + 10 * CHUNKS + 10
        sums = pl.pallas_call(
            functools.partial(kernel, n_blk, block, width),
            out_shape=jax.ShapeDtypeStruct((1, block), jnp.float32),
            in_specs=[pl.BlockSpec(memory_space=pl.ANY)],
            out_specs=pl.BlockSpec(memory_space=pltpu.VMEM),
            scratch_shapes=[
                pltpu.VMEM((8, block, width), jnp.bfloat16),
                pltpu.VMEM((block, width), jnp.bfloat16),
                pltpu.VMEM((block, width), jnp.bfloat16),
                pltpu.VMEM((block, width), jnp.bfloat16),
                pltpu.VMEM((8, 8, block), jnp.float32),
                pltpu.VMEM((8, 8, block), jnp.float32),
                pltpu.VMEM((8, block), jnp.float32),
                pltpu.VMEM((8, block), jnp.float32),
                pltpu.VMEM((9, 8, block), jnp.float32),
                pltpu.SemaphoreType.DMA,
                pltpu.SemaphoreType.DMA((n_sem,)),
                pltpu.SemaphoreType.DMA((n_sem,)),
            ],
            compiler_params=pltpu.CompilerParams(
                collective_id=0, has_side_effects=True, vmem_limit_bytes=40 * 2**20
            ),
            cost_estimate=pl.CostEstimate(flops=2 * 16 * block * block * width, bytes_accessed=2 * block * width,
                                          transcendentals=16 * block * block),
        )(embeddings)
        return sums.reshape(block)

    return jax.shard_map(
        body, mesh=mesh, in_specs=(P(("blk", "grp"), None),), out_specs=P(("blk", "grp")), check_vma=False
    )
```
